32 devices in a mesh: dp: 8 (over y, x, core), expert: 4 (over z).
Axes of the slice: x: 2, y: 2, z: 4, core: 2. Of those that a mesh axis runs over, the one named last changes fastest.
Arguments:
- tokens: bfloat16 [8192, 2048], P(('dp', 'expert')), may hold values from -6 to 6
- expert_ids: int32 [8192, 2], P(('dp', 'expert')), may hold values from 0 to 7, all different within a row; in each aligned block of 256 rows (0 to 255, 256 to 511, ...) at most 80 rows name the same one
- gate_weights: float32 [8192, 2], P(('dp', 'expert')), may hold values from 0.1 to 1
- old_place: int32 [8], replicated, may hold values from 0 to 7, each once
- new_place: int32 [8], replicated, may hold values from 0 to 7, each once
- params: bfloat16 [8, 3, 2048, 1024], P('dp', None, None, 'expert'), may hold values from -5 to 5
- grads: bfloat16 [8, 3, 2048, 1024], P('dp', None, None, 'expert'), may hold values from -6 to 6
- first_moment: float32 [8, 3, 2048, 1024], P('dp', None, None, 'expert'), may hold values from -2 to 2
- second_moment: float32 [8, 3, 2048, 1024], P('dp', None, None, 'expert'), may hold values from 0.05 to 1
Outputs:
- mixed: bfloat16 [8192, 2048], P(('dp', 'expert'))
- new_params: bfloat16 [8, 3, 2048, 1024], P('dp', None, None, 'expert')
- new_first: float32 [8, 3, 2048, 1024], P('dp', None, None, 'expert')
- new_second: float32 [8, 3, 2048, 1024], P('dp', None, None, 'expert')
The draws below stay inside these ranges and needn't reach their ends.
Inputs may be any that keep to these rules, and one draw needn't show every extreme that they name: `expert_ids`: each token names 2 different experts. Among the rows of one device no expert is named more than 80 times, and in every draw some device names some expert exactly 80 times. `old_place`: A permutation of the 8 experts. `new_place`: A permutation of the 8 experts.
All inputs are finite; a program needn't handle non-finite values.
Results may differ from the reference program's by a relative error of at most 0.0076.
Values may be sent and summed in bfloat16 or wider, within the bound.
A program may use at most 192 MiB of HBM per device.

```python
import math
import jax
import jax.numpy as jnp
import numpy as np
from jax import lax

D = 2048
FF = 1024
TOPK = 2
TOK_DEV = 256
EXPERTS = 8
TOKENS = 8192
CAP = 80


def steps_of(key, extent, cuts, low, top_value):
    factor_of, own = 1.0, jax.random.fold_in(key, 6)
    for axis_at, parts in cuts:
        steps = jnp.exp(jax.random.uniform(jax.random.fold_in(own, axis_at), (parts,), jnp.float32, low / len(cuts), top_value / len(cuts)))
        factor_of = factor_of * jnp.repeat(steps, extent[axis_at] // parts).reshape([-1 if axis == axis_at else 1 for axis in range(len(extent))])
    return factor_of


def shared_out(own_key, own, number, rows, count, top, most, lean):
    ranking = jax.random.permutation(own_key, count)
    packed, ordinary = shares(count, rows * top, most, lean, True), shares(count, rows * top, most, lean, False)
    places = jnp.arange(count)

    def named(tallies, turn):
        used = int((tallies > 0).sum())
        fixed = max(1, used // 4)
        moved = fixed + (places - fixed + turn * (used - fixed)) % max(1, count - fixed)
        return jnp.zeros((count,), jnp.int32).at[ranking[jnp.where(places < fixed, places, moved)]].set(jnp.asarray(tallies, jnp.int32))

    tallies = jnp.where(number % 4 == 0, named(packed, number // 4), named(ordinary, number - number // 4 - 1))
    mixed = jax.random.permutation(jax.random.fold_in(own, 3), count)
    source_of, receiver = mixed[0:count // 2 * 2:2], mixed[1:count // 2 * 2:2]
    margin = jnp.minimum(tallies[source_of] - 1, most - tallies[receiver]) // 2
    margin = jnp.where((source_of == ranking[0]) | (receiver == ranking[0]) | (tallies[receiver] == 0), 0, jnp.maximum(margin, 0))
    moved = jax.random.randint(jax.random.fold_in(own, 4), (count // 2,), 0, 1 << 20) % (margin + 1)
    tallies = tallies.at[source_of].add(-moved).at[receiver].add(moved)
    items = jnp.searchsorted(jnp.cumsum(tallies), jnp.arange(rows * top), side="right").astype(jnp.int32)
    listing = items.reshape(top, rows).T
    listing = listing[jax.random.permutation(jax.random.fold_in(own, 1), rows)]
    turn = jax.random.randint(jax.random.fold_in(own, 2), (rows, 1), 0, top)
    return jnp.take_along_axis(listing, (jnp.arange(top)[None, :] + turn) % top, axis=1)


def shares(count, total, most, skew, full):
    loads = [(1 << 20) // math.isqrt(rank ** skew) + 1 for rank in range(1, count + 1)]
    largest = most if full else min(most, max(-(-total // count), total * loads[0] // sum(loads)))
    least = 1 if total - largest >= count - 1 else 0
    counts, spare = [largest] + [least] * (count - 1), total - largest - least * (count - 1)
    while spare > 0:
        free = [i for i in range(1, count) if counts[i] < largest] or [i for i in range(1, count) if counts[i] < most]
        mass, left = sum([loads[i] for i in free]), spare
        for i in free:
            extra = min(most - counts[i], max(1, left * loads[i] // mass), spare)
            counts[i] = counts[i] + extra
            spare = spare - extra
    return np.array(counts)


def centred(key, extent, spread, reach, pieces=(), kind=jnp.bfloat16):
    values = spread * jax.random.normal(key, extent, jnp.float32)
    if pieces:
        values = values * steps_of(key, extent, pieces, -0.22, 0.18)
    return jnp.clip(values, -reach, reach).astype(kind)


def setup_inputs(seed: int = 0) -> dict:
    splits = jax.random.split(jax.random.key(seed), 10)
    tokens = centred(splits[0], (TOKENS, D), 1.0, 6.0, ((0, 32),))
    expert_ids_keys = jax.random.split(jax.random.fold_in(splits[1], 1), TOKENS // TOK_DEV)
    expert_ids_turns = jax.random.permutation(jax.random.fold_in(splits[1], 3), TOKENS // TOK_DEV)
    expert_ids = jax.vmap(lambda own, number: shared_out(jax.random.fold_in(splits[1], 2), own, number, TOK_DEV, EXPERTS, TOPK, CAP, 2))(expert_ids_keys, expert_ids_turns).reshape((TOKENS, TOPK))
    gate_weights = jnp.clip(0.1 + 0.9 * jax.random.uniform(splits[2], (TOKENS, TOPK), jnp.float32) ** steps_of(splits[2], (TOKENS, TOPK), ((0, 32),), -0.2, 0.2), 0.1, 1.0)
    old_place = jax.random.permutation(splits[3], EXPERTS).astype(jnp.int32)
    new_place = jax.random.permutation(splits[4], EXPERTS).astype(jnp.int32)
    params = centred(splits[5], (EXPERTS, 3, D, FF), 1.0, 5.0, ((0, 8), (3, 4)))
    grads = centred(splits[6], (EXPERTS, 3, D, FF), 1.0, 6.0, ((0, 8), (3, 4)))
    first_moment = centred(splits[7], (EXPERTS, 3, D, FF), 0.3, 2.0, ((0, 8), (3, 4)), jnp.float32)
    second_moment = jnp.clip(jnp.exp(math.log(1.0) - 2.9957323 * jax.random.uniform(splits[8], (EXPERTS, 3, D, FF), jnp.float32) ** steps_of(splits[8], (EXPERTS, 3, D, FF), ((0, 8), (3, 4)), -0.2, 0.2)), 0.05, 1.0)
    return {"tokens": tokens, "expert_ids": expert_ids, "gate_weights": gate_weights, "old_place": old_place, "new_place": new_place, "params": params, "grads": grads, "first_moment": first_moment, "second_moment": second_moment}


adam_rate = 0.3
first_decay = 0.9
second_decay = 0.95
adam_count = 10.0
adam_eps = 1e-08

def adam_update(params, grads, first_moment, second_moment):
    grad_value = grads.astype(jnp.float32)
    new_first = first_decay * first_moment + (1.0 - first_decay) * grad_value
    new_second = second_decay * second_moment + (1.0 - second_decay) * grad_value * grad_value
    first_hat = new_first / (1.0 - first_decay ** adam_count)
    second_hat = new_second / (1.0 - second_decay ** adam_count)
    stepped = params.astype(jnp.float32) - adam_rate * first_hat / (jnp.sqrt(second_hat) + adam_eps)
    return (stepped.astype(jnp.bfloat16), new_first, new_second)

def inverse_of(placement):
    entries = placement.shape[0]
    return jnp.zeros((entries,), jnp.int32).at[placement].set(jnp.arange(entries, dtype=jnp.int32))

def expert_forward(gathered_rows, weights):
    in_scale = 1.0 / math.sqrt(weights.shape[1])
    out_scale = 1.0 / math.sqrt(weights.shape[2])
    gate_part = jnp.dot(gathered_rows, weights[0], preferred_element_type=jnp.float32) * in_scale
    up_part = jnp.dot(gathered_rows, weights[1], preferred_element_type=jnp.float32) * in_scale
    hidden = (jax.nn.silu(gate_part) * up_part).astype(jnp.bfloat16)
    summed = lax.dot_general(hidden, weights[2], (((1,), (1,)), ((), ())), preferred_element_type=jnp.float32)
    return (summed * out_scale).astype(jnp.bfloat16)

def reference(tokens, expert_ids, gate_weights, old_place, new_place, params, grads, first_moment, second_moment):
    source = inverse_of(old_place)[new_place]
    new_params, new_first, new_second = adam_update(params[source], grads[source], first_moment[source], second_moment[source])
    blocks = tokens.shape[0] // TOK_DEV
    features = tokens.shape[1]
    routes = TOK_DEV * TOPK
    route_ids = expert_ids.reshape(blocks, routes)
    onehot = (route_ids[:, :, None] == jnp.arange(EXPERTS, dtype=jnp.int32)[None, None, :]).astype(jnp.int32)
    slot_rank = lax.optimization_barrier(jnp.sum((jnp.cumsum(onehot, axis=1) - 1) * onehot, axis=2))
    block_index = jnp.broadcast_to(jnp.arange(blocks, dtype=jnp.int32)[:, None], (blocks, routes))
    token_index = block_index * TOK_DEV + jnp.arange(routes, dtype=jnp.int32)[None, :] // TOPK
    flat_slot = ((route_ids * blocks + block_index) * CAP + slot_rank).reshape(-1)
    slot_token = jnp.full((EXPERTS * blocks * CAP,), -1, jnp.int32).at[flat_slot].set(token_index.reshape(-1))
    slot_gate = jnp.zeros((EXPERTS * blocks * CAP,), jnp.float32).at[flat_slot].set(gate_weights.reshape(-1))
    slot_token = slot_token.reshape(EXPERTS, blocks * CAP)
    slot_gate = slot_gate.reshape(EXPERTS, blocks * CAP)
    weight_row = inverse_of(new_place)

    def add_expert(running, expert):
        chosen = slot_token[expert]
        filled = chosen >= 0
        clamped = jnp.maximum(chosen, 0)
        gathered_rows = jnp.where(filled[:, None], tokens[clamped], jnp.zeros((), jnp.bfloat16))
        expert_out = expert_forward(gathered_rows, new_params[weight_row[expert]])
        weighted = expert_out.astype(jnp.float32) * slot_gate[expert][:, None]
        weighted = jnp.where(filled[:, None], weighted, jnp.zeros((), jnp.float32))
        return (running.at[clamped].add(weighted), None)
    running, unused = lax.scan(add_expert, jnp.zeros((tokens.shape[0], features), jnp.float32), jnp.arange(EXPERTS, dtype=jnp.int32))
    return (running.astype(jnp.bfloat16), new_params, new_first, new_second)
```

```python
import math

import jax
import jax.numpy as jnp
from jax import lax
from jax.sharding import PartitionSpec as P

FF = 1024


adam_rate = 0.3
first_decay = 0.9
second_decay = 0.95
adam_count = 10.0
adam_eps = 1e-08


def adam_update(params, grads, first_moment, second_moment):
    grad_value = grads.astype(jnp.float32)
    new_first = first_decay * first_moment + (1.0 - first_decay) * grad_value
    new_second = second_decay * second_moment + (1.0 - second_decay) * grad_value * grad_value
    first_hat = new_first / (1.0 - first_decay**adam_count)
    second_hat = new_second / (1.0 - second_decay**adam_count)
    stepped = params.astype(jnp.float32) - adam_rate * first_hat / (jnp.sqrt(second_hat) + adam_eps)
    return (stepped.astype(jnp.bfloat16), new_first, new_second)


def inverse_of(placement):
    entries = placement.shape[0]
    return jnp.zeros((entries,), jnp.int32).at[placement].set(jnp.arange(entries, dtype=jnp.int32))


def spread_blocks(value):
    pieces = lax.axis_size("dp")
    kinds, depth, width = value.shape
    return value.reshape(kinds, pieces, depth // pieces, width).transpose(1, 0, 2, 3)


def joined_blocks(blocks):
    pieces, kinds, depth, width = blocks.shape
    return blocks.transpose(1, 0, 2, 3).reshape(kinds, pieces * depth, width)


def relocate(blocks, source):
    spread = lax.all_to_all(blocks, "dp", split_axis=0, concat_axis=0, tiled=True)
    return lax.all_to_all(spread[source], "dp", split_axis=0, concat_axis=0, tiled=True)


def local(
    tokens,
    expert_ids,
    gate_weights,
    old_place,
    new_place,
    params,
    grads,
    first_moment,
    second_moment,
):
    experts = old_place.shape[0]
    tok_rows, features = tokens.shape
    topk = expert_ids.shape[1]
    capacity = 5 * tok_rows * topk // (4 * experts)
    source = inverse_of(old_place)[new_place]
    own_params, own_first, own_second = adam_update(
        params[0], grads[0], first_moment[0], second_moment[0]
    )
    moved_params = relocate(spread_blocks(own_params), source)
    moments = jnp.concatenate(
        [
            spread_blocks(own_first.astype(jnp.bfloat16)),
            spread_blocks(own_second.astype(jnp.bfloat16)),
        ],
        axis=1,
    )
    moved_moments = relocate(moments, source)
    new_params = joined_blocks(moved_params)[None]
    kinds = params.shape[1]
    new_first = joined_blocks(moved_moments[:, :kinds]).astype(jnp.float32)[None]
    new_second = joined_blocks(moved_moments[:, kinds:]).astype(jnp.float32)[None]
    flat_ids = expert_ids.reshape(-1)
    onehot = (flat_ids[:, None] == jnp.arange(experts, dtype=jnp.int32)[None, :]).astype(jnp.int32)
    slot_rank = jnp.sum((jnp.cumsum(onehot, axis=0) - 1) * onehot, axis=1)
    route_row = inverse_of(new_place)[flat_ids]
    slot_index = route_row * capacity + slot_rank
    slot_token = (
        jnp.full((experts * capacity,), -1, jnp.int32)
        .at[slot_index]
        .set(jnp.arange(flat_ids.shape[0], dtype=jnp.int32) // topk)
    )
    filled = slot_token >= 0
    outgoing = jnp.where(
        filled[:, None], tokens[jnp.maximum(slot_token, 0)], jnp.zeros((), jnp.bfloat16)
    )
    arrived = lax.all_to_all(
        outgoing.reshape(experts, capacity, features), "dp", split_axis=0, concat_axis=0, tiled=True
    ).reshape(-1, features)
    in_scale = 1.0 / math.sqrt(features)
    out_scale = 1.0 / math.sqrt(FF)
    columns = lax.all_gather(new_params[0], "expert", axis=2, tiled=True)
    gate_part = jnp.dot(arrived, columns[0], preferred_element_type=jnp.float32) * in_scale
    up_part = jnp.dot(arrived, columns[1], preferred_element_type=jnp.float32) * in_scale
    hidden = (jax.nn.silu(gate_part) * up_part).astype(jnp.bfloat16)
    summed = lax.dot_general(
        hidden, columns[2], (((1,), (1,)), ((), ())), preferred_element_type=jnp.float32
    )
    expert_out = (summed * out_scale).astype(jnp.bfloat16)
    returned = lax.all_to_all(
        expert_out.reshape(experts, capacity, features),
        "dp",
        split_axis=0,
        concat_axis=0,
        tiled=True,
    ).reshape(-1, features)
    picked = returned[slot_index].astype(jnp.float32).reshape(tok_rows, topk, features)
    mixed_out = jnp.sum(picked * gate_weights[:, :, None], axis=1).astype(jnp.bfloat16)
    return (mixed_out, new_params, new_first, new_second)


def solution(mesh):
    return jax.shard_map(
        local,
        mesh=mesh,
        in_specs=(
            P(("dp", "expert"), None),
            P(("dp", "expert"), None),
            P(("dp", "expert"), None),
            P(),
            P(),
            P("dp", None, None, "expert"),
            P("dp", None, None, "expert"),
            P("dp", None, None, "expert"),
            P("dp", None, None, "expert"),
        ),
        out_specs=(
            P(("dp", "expert"), None),
            P("dp", None, None, "expert"),
            P("dp", None, None, "expert"),
            P("dp", None, None, "expert"),
        ),
        check_vma=False,
    )
```

```python
import functools
import math

import jax
import jax.numpy as jnp
from jax import lax
from jax.experimental import pallas as pl
from jax.experimental.pallas import tpu as pltpu
from jax.sharding import PartitionSpec as P

adam_rate = 0.3
first_decay = 0.9
second_decay = 0.95
adam_count = 10.0
adam_eps = 1e-08


def adam_update(params, grads, first_moment, second_moment):
    grad_value = grads.astype(jnp.float32)
    new_first = first_decay * first_moment + (1.0 - first_decay) * grad_value
    new_second = second_decay * second_moment + (1.0 - second_decay) * grad_value * grad_value
    first_hat = new_first / (1.0 - first_decay**adam_count)
    second_hat = new_second / (1.0 - second_decay**adam_count)
    stepped = params.astype(jnp.float32) - adam_rate * first_hat / (jnp.sqrt(second_hat) + adam_eps)
    return (stepped.astype(jnp.bfloat16), new_first, new_second)


def inverse_of(placement):
    number = jnp.arange(placement.shape[0], dtype=jnp.int32)
    return jnp.sum(jnp.where(placement[:, None] == number[None, :], number[:, None], 0), axis=0)


def swap(blocks):
    return lax.all_to_all(blocks, "dp", split_axis=0, concat_axis=0, tiled=True)


def move_kernel(
    rows_dp,
    shards,
    kinds,
    source,
    params,
    first,
    second,
    outgoing,
    weights,
    new_first,
    new_second,
    arrived,
    *scratch,
):
    chunks = 3 * kinds
    caught, sorted_ = scratch[:chunks], scratch[chunks : 2 * chunks]
    (one_send, one_recv, two_send, two_recv, own_sem, tok_send, tok_recv, z_send, z_recv) = scratch[
        2 * chunks :
    ]
    me, z = lax.axis_index("dp"), lax.axis_index("expert")
    block = params.shape[1] // rows_dp
    has_left, has_right = z > 0, z < shards - 1

    def rows(row):
        return pl.ds(pl.multiple_of(row * block, block), block)

    def remote(src, dst, send, recv, target):
        return pltpu.make_async_remote_copy(
            src_ref=src,
            dst_ref=dst,
            send_sem=send,
            recv_sem=recv,
            device_id=target,
            device_id_type=pl.DeviceIdType.MESH,
        )

    def peers(body):
        def step(offset, carry):
            body(lax.rem(me + offset, rows_dp))
            return carry

        lax.fori_loop(1, rows_dp, step, 0)

    def origin(chunk, row):
        return (params, first, second)[chunk // kinds].at[chunk % kinds, rows(row)]

    def final(chunk, row):
        if chunk < kinds:
            return weights.at[chunk, z, rows(row)]
        return (new_first, new_second)[chunk // kinds - 1].at[chunk % kinds, rows(row)]

    def one(chunk, peer, sender):
        return remote(
            origin(chunk, peer),
            caught[chunk].at[sender],
            one_send.at[chunk, peer],
            one_recv.at[chunk, sender],
            {"dp": peer},
        )

    def one_own(chunk):
        return pltpu.make_async_copy(
            origin(chunk, me), caught[chunk].at[me], own_sem.at[0, chunk]
        )

    def two(chunk, peer, sender):
        return remote(
            sorted_[chunk].at[peer],
            final(chunk, sender),
            two_send.at[chunk, peer],
            two_recv.at[chunk, sender],
            {"dp": peer},
        )

    def two_own(chunk):
        return pltpu.make_async_copy(
            sorted_[chunk].at[me], final(chunk, me), own_sem.at[1, chunk]
        )

    def tok(peer, sender):
        return remote(
            outgoing.at[peer],
            arrived.at[sender],
            tok_send.at[peer],
            tok_recv.at[sender],
            {"dp": peer},
        )

    def tok_own():
        return pltpu.make_async_copy(outgoing.at[me], arrived.at[me], tok_send.at[me])

    def along(kind, shard, way):
        return remote(
            weights.at[kind, shard],
            weights.at[kind, shard],
            z_send.at[kind, shard, way],
            z_recv.at[kind, shard],
            {"expert": z + (1 if way == 0 else -1)},
        )

    def start_one(chunk):
        one_own(chunk).start()
        peers(lambda peer: one(chunk, peer, me).start())

    def turn(chunk):
        one_own(chunk).wait()
        peers(lambda peer: one(chunk, peer, peer).wait_recv())

        def pick(row, carry):
            sorted_[chunk][row] = caught[chunk][source[row]]
            return carry

        lax.fori_loop(0, rows_dp, pick, 0)
        two_own(chunk).start()
        peers(lambda peer: two(chunk, peer, me).start())

    def finish_two(chunk):
        two_own(chunk).wait()
        peers(lambda peer: two(chunk, peer, peer).wait_recv())

    def z_own(kind):
        @pl.when(has_right)
        def _():
            along(kind, z, 0).start()

        @pl.when(has_left)
        def _():
            along(kind, z, 1).start()

    def z_step(kind, step):
        @pl.when(z - 1 - step >= 0)
        def _():
            along(kind, z - 1 - step, 0).wait_recv()

            @pl.when(has_right)
            def _():
                along(kind, z - 1 - step, 0).start()

        @pl.when(z + 1 + step < shards)
        def _():
            along(kind, z + 1 + step, 1).wait_recv()

            @pl.when(has_left)
            def _():
                along(kind, z + 1 + step, 1).start()

    def z_sent(kind, step):
        @pl.when(jnp.logical_and(z - step >= 0, has_right))
        def _():
            along(kind, z - step, 0).wait_send()

        @pl.when(jnp.logical_and(z + step < shards, has_left))
        def _():
            along(kind, z + step, 1).wait_send()

    barrier = pltpu.get_barrier_semaphore()

    def greet(target):
        pl.semaphore_signal(
            barrier, inc=1, device_id=target, device_id_type=pl.DeviceIdType.MESH
        )

    peers(lambda peer: greet({"dp": peer}))

    @pl.when(has_left)
    def _():
        greet({"expert": z - 1})

    @pl.when(has_right)
    def _():
        greet({"expert": z + 1})

    pl.semaphore_wait(
        barrier, rows_dp - 1 + has_left.astype(jnp.int32) + has_right.astype(jnp.int32)
    )

    started = 2
    for chunk in range(started):
        start_one(chunk)
    last = max(chunks + 1, kinds + 2 * shards)
    for tick in range(last):
        if tick < chunks:
            turn(tick)
        while started < min(chunks, tick + (3 if tick < kinds - 1 else 4)):
            start_one(started)
            started += 1
        if tick == kinds - 1:
            tok_own().start()
            peers(lambda peer: tok(peer, me).start())
        if 1 <= tick <= chunks:
            finish_two(tick - 1)
            if tick - 1 < kinds:
                z_own(tick - 1)
        for kind in range(kinds):
            step, odd = divmod(tick - kind - 2, 2)
            if odd == 0 and 0 <= step < shards - 1:
                z_step(kind, step)

    tok_own().wait()
    peers(lambda peer: tok(peer, peer).wait_recv())
    peers(lambda peer: tok(peer, me).wait_send())
    for chunk in range(chunks):
        peers(lambda peer: one(chunk, peer, me).wait_send())
        peers(lambda peer: two(chunk, peer, me).wait_send())
    for kind in range(kinds):
        for step in range(shards - 1):
            z_sent(kind, step)


def move(source, params, first, second, outgoing):
    kinds, depth, width = params.shape
    rows_dp, shards = lax.axis_size("dp"), lax.axis_size("expert")
    chunks = 3 * kinds
    held = pltpu.VMEM((rows_dp, depth // rows_dp, width), jnp.bfloat16)
    dma = pltpu.SemaphoreType.DMA
    state = jax.ShapeDtypeStruct(params.shape, jnp.bfloat16)
    anywhere = pl.BlockSpec(memory_space=pl.ANY)
    return pl.pallas_call(
        functools.partial(move_kernel, rows_dp, shards, kinds),
        out_shape=(
            jax.ShapeDtypeStruct((kinds, shards, depth, width), jnp.bfloat16),
            state,
            state,
            jax.ShapeDtypeStruct(outgoing.shape, jnp.bfloat16),
        ),
        in_specs=[pl.BlockSpec(memory_space=pltpu.SMEM)] + [anywhere] * 4,
        out_specs=(anywhere,) * 4,
        scratch_shapes=[held] * (2 * chunks)
        + [dma((chunks, rows_dp))] * 4
        + [
            dma((2, chunks)),
            dma((rows_dp,)),
            dma((rows_dp,)),
            dma((kinds, shards, 2)),
            dma((kinds, shards)),
        ],
        compiler_params=pltpu.CompilerParams(
            collective_id=0, has_side_effects=True, vmem_limit_bytes=44 * 1024 * 1024
        ),
    )(source, params, first, second, outgoing)


def local(
    tokens,
    expert_ids,
    gate_weights,
    old_place,
    new_place,
    params,
    grads,
    first_moment,
    second_moment,
):
    experts = old_place.shape[0]
    tok_rows, features = tokens.shape
    topk = expert_ids.shape[1]
    routes = tok_rows * topk
    capacity = 5 * routes // (4 * experts)
    slots = experts * capacity
    kinds, depth, width = params.shape[1:]
    shards = lax.axis_size("expert")
    half = features // 2
    source = inverse_of(old_place)[new_place]

    own_params, own_first, own_second = adam_update(
        params[0], grads[0], first_moment[0], second_moment[0]
    )

    flat_ids = expert_ids.reshape(-1)
    onehot = (flat_ids[:, None] == jnp.arange(experts, dtype=jnp.int32)[None, :])
    order = jnp.arange(routes, dtype=jnp.int32)
    earlier = (order[:, None] > order[None, :]).astype(jnp.bfloat16)
    counts = jnp.dot(earlier, onehot.astype(jnp.bfloat16), preferred_element_type=jnp.float32)
    slot_rank = jnp.sum(jnp.where(onehot, counts, 0.0), axis=1).astype(jnp.int32)
    row_of = inverse_of(new_place)
    route_row = jnp.sum(jnp.where(onehot, row_of[None, :], 0), axis=1)
    slot_index = (route_row * capacity + slot_rank).reshape(tok_rows, topk)
    slot_number = jnp.arange(slots, dtype=jnp.int32)
    hits = [slot_index[:, k, None] == slot_number[None, :] for k in range(topk)]
    chosen = sum(hit.astype(jnp.bfloat16) for hit in hits)
    mixing = sum(
        jnp.where(hits[k], gate_weights[:, k, None], 0.0) for k in range(topk)
    )
    mixing_high = mixing.astype(jnp.bfloat16)
    mixing_low = (mixing - mixing_high.astype(jnp.float32)).astype(jnp.bfloat16)

    outgoing = lax.dot_general(
        chosen, tokens, (((0,), (0,)), ((), ())), preferred_element_type=jnp.float32
    ).astype(jnp.bfloat16)
    weights, moved_first, moved_second, arrived = move(
        source,
        own_params,
        own_first.astype(jnp.bfloat16),
        own_second.astype(jnp.bfloat16),
        outgoing.reshape(experts, capacity, features),
    )
    arrived = arrived.reshape(slots, features)
    new_params = lax.dynamic_index_in_dim(
        weights, lax.axis_index("expert"), axis=1, keepdims=False
    )[None]
    new_first = moved_first.astype(jnp.float32)[None]
    new_second = moved_second.astype(jnp.float32)[None]

    in_scale = 1.0 / math.sqrt(features)
    out_scale = 1.0 / math.sqrt(width * shards)

    def into(kind):
        return [
            jnp.dot(arrived, weights[kind, z], preferred_element_type=jnp.float32) * in_scale
            for z in range(shards)
        ]

    gate_part, up_part = into(0), into(1)
    hidden = [
        (jax.nn.silu(gate) * up).astype(jnp.bfloat16) for gate, up in zip(gate_part, up_part)
    ]
    mixed = []
    for start in (0, half):
        summed = sum(
            lax.dot_general(
                hidden[z],
                weights[2, z, start : start + half],
                (((1,), (1,)), ((), ())),
                preferred_element_type=jnp.float32,
            )
            for z in range(shards)
        )
        expert_out = (summed * out_scale).astype(jnp.bfloat16)
        returned = swap(expert_out.reshape(experts, capacity, -1)).reshape(slots, -1)
        total = jnp.dot(mixing_high, returned, preferred_element_type=jnp.float32)
        total += jnp.dot(mixing_low, returned, preferred_element_type=jnp.float32)
        mixed.append(total.astype(jnp.bfloat16))
    return (jnp.concatenate(mixed, axis=1), new_params, new_first, new_second)


def solution(mesh):
    row, state = P(("dp", "expert"), None), P("dp", None, None, "expert")
    return jax.shard_map(
        local,
        mesh=mesh,
        in_specs=(row, row, row, P(), P(), state, state, state, state),
        out_specs=(row, state, state, state),
        check_vma=False,
    )
```

```python
import functools
import math

import jax
import jax.numpy as jnp
from jax import lax
from jax.experimental import pallas as pl
from jax.experimental.pallas import tpu as pltpu
from jax.sharding import PartitionSpec as P

adam_rate = 0.3
first_decay = 0.9
second_decay = 0.95
adam_count = 10.0
adam_eps = 1e-08


def adam_update(params, grads, first_moment, second_moment):
    grad_value = grads.astype(jnp.float32)
    new_first = first_decay * first_moment + (1.0 - first_decay) * grad_value
    new_second = second_decay * second_moment + (1.0 - second_decay) * grad_value * grad_value
    first_hat = new_first / (1.0 - first_decay**adam_count)
    second_hat = new_second / (1.0 - second_decay**adam_count)
    stepped = params.astype(jnp.float32) - adam_rate * first_hat / (jnp.sqrt(second_hat) + adam_eps)
    return (stepped.astype(jnp.bfloat16), new_first, new_second)


def inverse_of(placement):
    number = jnp.arange(placement.shape[0], dtype=jnp.int32)
    return jnp.sum(jnp.where(placement[:, None] == number[None, :], number[:, None], 0), axis=0)


def swap(blocks):
    return lax.all_to_all(blocks, "dp", split_axis=0, concat_axis=0, tiled=True)


def move_kernel(
    rows_dp,
    shards,
    kinds,
    source,
    params,
    first,
    second,
    outgoing,
    weights,
    new_first,
    new_second,
    arrived,
    *scratch,
):
    chunks = 3 * kinds
    caught, sorted_ = scratch[:chunks], scratch[chunks : 2 * chunks]
    (one_send, one_recv, two_send, two_recv, own_sem, tok_send, tok_recv, z_send, z_recv) = scratch[
        2 * chunks :
    ]
    me, z = lax.axis_index("dp"), lax.axis_index("expert")
    block = params.shape[1] // rows_dp
    has_left, has_right = z > 0, z < shards - 1

    def rows(row):
        return pl.ds(pl.multiple_of(row * block, block), block)

    def columns(shard):
        width = params.shape[2]
        return pl.ds(pl.multiple_of(shard * width, width), width)

    def remote(src, dst, send, recv, target):
        return pltpu.make_async_remote_copy(
            src_ref=src,
            dst_ref=dst,
            send_sem=send,
            recv_sem=recv,
            device_id=target,
            device_id_type=pl.DeviceIdType.MESH,
        )

    def peers(body):
        def step(offset, carry):
            body(lax.rem(me + offset, rows_dp))
            return carry

        lax.fori_loop(1, rows_dp, step, 0)

    def origin(chunk, row):
        return (params, first, second)[chunk // kinds].at[chunk % kinds, rows(row)]

    def final(chunk, row):
        if chunk < kinds:
            return weights.at[chunk, rows(row), columns(z)]
        return (new_first, new_second)[chunk // kinds - 1].at[chunk % kinds, rows(row)]

    def one(chunk, peer, sender):
        return remote(
            origin(chunk, peer),
            caught[chunk].at[sender],
            one_send.at[chunk, peer],
            one_recv.at[chunk, sender],
            {"dp": peer},
        )

    def one_own(chunk):
        return pltpu.make_async_copy(
            origin(chunk, me), caught[chunk].at[me], own_sem.at[0, chunk]
        )

    def two(chunk, peer, sender):
        return remote(
            sorted_[chunk].at[peer],
            final(chunk, sender),
            two_send.at[chunk, peer],
            two_recv.at[chunk, sender],
            {"dp": peer},
        )

    def two_own(chunk):
        return pltpu.make_async_copy(
            sorted_[chunk].at[me], final(chunk, me), own_sem.at[1, chunk]
        )

    def tok(peer, sender):
        return remote(
            outgoing.at[peer],
            arrived.at[sender],
            tok_send.at[peer],
            tok_recv.at[sender],
            {"dp": peer},
        )

    def tok_own():
        return pltpu.make_async_copy(outgoing.at[me], arrived.at[me], tok_send.at[me])

    def along(kind, shard, way):
        return remote(
            weights.at[kind, :, columns(shard)],
            weights.at[kind, :, columns(shard)],
            z_send.at[kind, shard, way],
            z_recv.at[kind, shard],
            {"expert": z + (1 if way == 0 else -1)},
        )

    def start_one(chunk):
        one_own(chunk).start()
        peers(lambda peer: one(chunk, peer, me).start())

    def turn(chunk):
        one_own(chunk).wait()
        peers(lambda peer: one(chunk, peer, peer).wait_recv())

        def pick(row, carry):
            sorted_[chunk][row] = caught[chunk][source[row]]
            return carry

        lax.fori_loop(0, rows_dp, pick, 0)
        two_own(chunk).start()
        peers(lambda peer: two(chunk, peer, me).start())

    def finish_two(chunk):
        two_own(chunk).wait()
        peers(lambda peer: two(chunk, peer, peer).wait_recv())

    def z_own(kind):
        @pl.when(has_right)
        def _():
            along(kind, z, 0).start()

        @pl.when(has_left)
        def _():
            along(kind, z, 1).start()

    def z_step(kind, step):
        @pl.when(z - 1 - step >= 0)
        def _():
            along(kind, z - 1 - step, 0).wait_recv()

            @pl.when(has_right)
            def _():
                along(kind, z - 1 - step, 0).start()

        @pl.when(z + 1 + step < shards)
        def _():
            along(kind, z + 1 + step, 1).wait_recv()

            @pl.when(has_left)
            def _():
                along(kind, z + 1 + step, 1).start()

    def z_sent(kind, step):
        @pl.when(jnp.logical_and(z - step >= 0, has_right))
        def _():
            along(kind, z - step, 0).wait_send()

        @pl.when(jnp.logical_and(z + step < shards, has_left))
        def _():
            along(kind, z + step, 1).wait_send()

    barrier = pltpu.get_barrier_semaphore()

    def greet(target):
        pl.semaphore_signal(
            barrier, inc=1, device_id=target, device_id_type=pl.DeviceIdType.MESH
        )

    peers(lambda peer: greet({"dp": peer}))

    @pl.when(has_left)
    def _():
        greet({"expert": z - 1})

    @pl.when(has_right)
    def _():
        greet({"expert": z + 1})

    pl.semaphore_wait(
        barrier, rows_dp - 1 + has_left.astype(jnp.int32) + has_right.astype(jnp.int32)
    )

    started = 2
    for chunk in range(started):
        start_one(chunk)
    last = max(chunks + 1, kinds + 2 * shards)
    for tick in range(last):
        if tick < chunks:
            turn(tick)
        while started < min(chunks, tick + (3 if tick < kinds - 1 else 4)):
            start_one(started)
            started += 1
        if tick == kinds - 1:
            tok_own().start()
            peers(lambda peer: tok(peer, me).start())
        if 1 <= tick <= chunks:
            finish_two(tick - 1)
            if tick - 1 < kinds:
                z_own(tick - 1)
        for kind in range(kinds):
            step, odd = divmod(tick - kind - 2, 2)
            if odd == 0 and 0 <= step < shards - 1:
                z_step(kind, step)

    tok_own().wait()
    peers(lambda peer: tok(peer, peer).wait_recv())
    peers(lambda peer: tok(peer, me).wait_send())
    for chunk in range(chunks):
        peers(lambda peer: one(chunk, peer, me).wait_send())
        peers(lambda peer: two(chunk, peer, me).wait_send())
    for kind in range(kinds):
        for step in range(shards - 1):
            z_sent(kind, step)


def move(source, params, first, second, outgoing):
    kinds, depth, width = params.shape
    rows_dp, shards = lax.axis_size("dp"), lax.axis_size("expert")
    chunks = 3 * kinds
    held = pltpu.VMEM((rows_dp, depth // rows_dp, width), jnp.bfloat16)
    dma = pltpu.SemaphoreType.DMA
    state = jax.ShapeDtypeStruct(params.shape, jnp.bfloat16)
    anywhere = pl.BlockSpec(memory_space=pl.ANY)
    return pl.pallas_call(
        functools.partial(move_kernel, rows_dp, shards, kinds),
        out_shape=(
            jax.ShapeDtypeStruct((kinds, depth, width * shards), jnp.bfloat16),
            state,
            state,
            jax.ShapeDtypeStruct(outgoing.shape, jnp.bfloat16),
        ),
        in_specs=[pl.BlockSpec(memory_space=pltpu.SMEM)] + [anywhere] * 4,
        out_specs=(anywhere,) * 4,
        scratch_shapes=[held] * (2 * chunks)
        + [dma((chunks, rows_dp))] * 4
        + [
            dma((2, chunks)),
            dma((rows_dp,)),
            dma((rows_dp,)),
            dma((kinds, shards, 2)),
            dma((kinds, shards)),
        ],
        compiler_params=pltpu.CompilerParams(
            collective_id=0, has_side_effects=True, vmem_limit_bytes=44 * 1024 * 1024
        ),
    )(source, params, first, second, outgoing)


def local(
    tokens,
    expert_ids,
    gate_weights,
    old_place,
    new_place,
    params,
    grads,
    first_moment,
    second_moment,
):
    experts = old_place.shape[0]
    tok_rows, features = tokens.shape
    topk = expert_ids.shape[1]
    routes = tok_rows * topk
    capacity = 5 * routes // (4 * experts)
    slots = experts * capacity
    kinds, depth, width = params.shape[1:]
    shards = lax.axis_size("expert")
    source = inverse_of(old_place)[new_place]

    own_params, own_first, own_second = adam_update(
        params[0], grads[0], first_moment[0], second_moment[0]
    )

    flat_ids = expert_ids.reshape(-1)
    onehot = (flat_ids[:, None] == jnp.arange(experts, dtype=jnp.int32)[None, :])
    order = jnp.arange(routes, dtype=jnp.int32)
    earlier = (order[:, None] > order[None, :]).astype(jnp.bfloat16)
    counts = jnp.dot(earlier, onehot.astype(jnp.bfloat16), preferred_element_type=jnp.float32)
    slot_rank = jnp.sum(jnp.where(onehot, counts, 0.0), axis=1).astype(jnp.int32)
    row_of = inverse_of(new_place)
    route_row = jnp.sum(jnp.where(onehot, row_of[None, :], 0), axis=1)
    slot_index = (route_row * capacity + slot_rank).reshape(tok_rows, topk)
    slot_number = jnp.arange(slots, dtype=jnp.int32)
    hits = [slot_index[:, k, None] == slot_number[None, :] for k in range(topk)]
    chosen = sum(hit.astype(jnp.bfloat16) for hit in hits)
    mixing = sum(
        jnp.where(hits[k], gate_weights[:, k, None], 0.0) for k in range(topk)
    )
    mixing_high = lax.reduce_precision(mixing, 8, 7).astype(jnp.bfloat16)
    mixing_low = (mixing - mixing_high.astype(jnp.float32)).astype(jnp.bfloat16)

    outgoing = lax.dot_general(
        chosen, tokens, (((0,), (0,)), ((), ())), preferred_element_type=jnp.float32
    ).astype(jnp.bfloat16)
    weights, moved_first, moved_second, arrived = move(
        source,
        own_params,
        own_first.astype(jnp.bfloat16),
        own_second.astype(jnp.bfloat16),
        outgoing.reshape(experts, capacity, features),
    )
    arrived = arrived.reshape(slots, features)
    new_params = lax.dynamic_slice_in_dim(
        weights, lax.axis_index("expert") * width, width, axis=2
    )[None]
    new_first = moved_first.astype(jnp.float32)[None]
    new_second = moved_second.astype(jnp.float32)[None]

    in_scale = 1.0 / math.sqrt(features)
    out_scale = 1.0 / math.sqrt(width * shards)

    middle = features // 2
    gate_part = jnp.dot(arrived, weights[0], preferred_element_type=jnp.float32) * in_scale
    up_part = jnp.dot(arrived, weights[1], preferred_element_type=jnp.float32) * in_scale
    hidden = (jax.nn.silu(gate_part) * up_part).astype(jnp.bfloat16)
    expert_out = jnp.concatenate(
        [
            (
                lax.dot_general(
                    hidden,
                    weights[2, start : start + middle],
                    (((1,), (1,)), ((), ())),
                    preferred_element_type=jnp.float32,
                )
                * out_scale
            ).astype(jnp.bfloat16)
            for start in (0, middle)
        ],
        axis=1,
    )
    returned = swap(expert_out.reshape(experts, capacity, features)).reshape(slots, features)
    mixed = jnp.dot(mixing_high, returned, preferred_element_type=jnp.float32)
    mixed += jnp.dot(mixing_low, returned, preferred_element_type=jnp.float32)
    return (mixed.astype(jnp.bfloat16), new_params, new_first, new_second)


def solution(mesh):
    row, state = P(("dp", "expert"), None), P("dp", None, None, "expert")
    return jax.shard_map(
        local,
        mesh=mesh,
        in_specs=(row, row, row, P(), P(), state, state, state, state),
        out_specs=(row, state, state, state),
        check_vma=False,
    )
```
